512 devices in a mesh: lat: 64 (over z, x_lo, core), tok: 8 (over x_hi, y).
Axes of the slice: x: 4 (x_hi: 2, x_lo: 2; x = x_hi * 2 + x_lo), y: 4, z: 16, core: 2. Of those that a mesh axis runs over, the one named last changes fastest.
Arguments:
- inputs: bfloat16 [512, 4096], P('lat', 'tok'), may hold values from -6 to 6
- targets: bfloat16 [512, 4096], P('lat', 'tok'), may hold values from -24 to 24
- enc_weight: bfloat16 [4096, 65536], P('tok', 'lat'), may hold values from -0.09375 to 0.09375
- enc_bias: float32 [65536], P('lat'), may hold values from -3 to 3
- dec_weight: bfloat16 [65536, 4096], P('lat', 'tok'), may hold values from -0.0234375 to 0.0234375
- dec_bias: float32 [4096], P('tok'), may hold values from -3 to 3
Outputs:
- loss: float32 [], replicated
- grad_enc: bfloat16 [4096, 65536], P('tok', 'lat')
- grad_dec: bfloat16 [65536, 4096], P('lat', 'tok')
- grad_enc_bias: float32 [65536], P('lat')
- grad_dec_bias: float32 [4096], P('tok')
The draws below stay inside these ranges and needn't reach their ends.
All inputs are finite; a program needn't handle non-finite values.
Results may differ from the reference program's by a relative error of at most 0.04.
Values may be sent and summed in bfloat16 or wider, within the bound.
No kernel may reach another device: no remote copies, remote signals or barrier semaphores. Data moves between devices by JAX's collectives and lax.ppermute only.
A program may use at most 64 MiB of HBM per device.

```python
import math
import jax
import jax.numpy as jnp
from jax import lax

D = 4096
LATENTS = 65536
TOKENS = 512
N_TOK = 8


def draw_targets(key, part):
    key = jax.random.fold_in(key, 11)
    noise_key = jax.random.fold_in(key, 0)
    column = jnp.arange(D, dtype=jnp.float32) / (D - 1)
    values = jnp.clip(jax.random.normal(noise_key, (TOKENS, D), jnp.float32), -6.0, 6.0)
    scaled = values * jnp.exp(jnp.log(4.0) * column)
    return jnp.clip(scaled, -24.0, 24.0).astype(jnp.bfloat16)


def levels(key, shape, cuts, low, largest):
    level = 1.0
    for dim, shards_of in cuts:
        heights = jax.random.uniform(jax.random.fold_in(jax.random.fold_in(key, 6), dim), (shards_of,), jnp.float32, low / len(cuts), largest / len(cuts))
        level = level * jnp.repeat(jnp.exp(heights), shape[dim] // shards_of).reshape((-1,) + (1,) * (len(shape) - 1 - dim))
    return level


def scatter_about(own_key, shape, deviation, most, cuts=(), kind=jnp.bfloat16):
    loudness = levels(own_key, shape, cuts, -0.22, 0.18) if cuts else 1.0
    values = jax.random.normal(own_key, shape, jnp.float32) * deviation * loudness
    return jnp.minimum(jnp.maximum(values, -most), most).astype(kind)


def setup_inputs(seed: int = 0) -> dict:
    streams_of = jax.random.split(jax.random.key(seed), 7)
    return {
        "inputs": scatter_about(streams_of[0], (TOKENS, D), 1.0, 6.0, ((0, 64), (1, 8))),
        "targets": draw_targets(jax.random.fold_in(streams_of[6], 71), 0),
        "enc_weight": scatter_about(streams_of[2], (D, LATENTS), D ** -0.5, 0.09375, ((0, 8), (1, 64))),
        "enc_bias": scatter_about(streams_of[3], (LATENTS,), 0.5, 3.0, ((0, 64),), jnp.float32),
        "dec_weight": scatter_about(streams_of[4], (LATENTS, D), LATENTS ** -0.5, 0.0234375, ((0, 64), (1, 8))),
        "dec_bias": scatter_about(streams_of[5], (D,), 0.5, 3.0, ((0, 8),), jnp.float32),
    }


sparsity = 0.03

def grouped(left_side, right_side):
    width = left_side.shape[1] // N_TOK
    total = jnp.zeros((left_side.shape[0], right_side.shape[1]), jnp.float32)
    for feature_block in range(N_TOK):
        lower = feature_block * width
        partial_value = jnp.dot(left_side[:, lower:lower + width], right_side[lower:lower + width], preferred_element_type=jnp.float32)
        rounded = lax.optimization_barrier(partial_value.astype(jnp.bfloat16))
        total = total + rounded.astype(jnp.float32)
    return total

def reference(inputs, targets, enc_weight, enc_bias, dec_weight, dec_bias):
    scale_root = math.sqrt(TOKENS)
    preact = grouped(inputs, enc_weight) + enc_bias
    lifted = jnp.maximum(preact, 0.0)
    latent = lifted * lifted
    latent_low = latent.astype(jnp.bfloat16)
    recon = jnp.dot(latent_low, dec_weight, preferred_element_type=jnp.float32) + dec_bias
    residual = recon - targets.astype(jnp.float32)
    loss = (0.5 * jnp.sum(residual * residual) + sparsity * jnp.sum(latent)) / (TOKENS * D)
    grad_recon = (residual / scale_root).astype(jnp.bfloat16)
    grad_dec_bias = lax.optimization_barrier(jnp.sum(grad_recon.astype(jnp.float32), axis=0))
    grad_dec = jnp.dot(latent_low.T, grad_recon, preferred_element_type=jnp.float32).astype(jnp.bfloat16)
    back_grad = grouped(grad_recon, dec_weight.T) + sparsity / scale_root
    grad_pre = back_grad * (2.0 * lifted)
    grad_enc_bias = lax.optimization_barrier(jnp.sum(grad_pre, axis=0))
    grad_enc = jnp.dot(inputs.T, grad_pre.astype(jnp.bfloat16), preferred_element_type=jnp.float32).astype(jnp.bfloat16)
    return (loss, grad_enc, grad_dec, grad_enc_bias, grad_dec_bias)
```

```python
import math

import jax
import jax.numpy as jnp
from jax import lax
from jax.sharding import Mesh, PartitionSpec as P

sparsity = 0.03

Z, XL, C, XH, Y = 16, 2, 2, 2, 4
LAT = ("z", "xl", "c")
TOK = ("xh", "y")
N_TOK = XH * Y
bf16, f32 = jnp.bfloat16, jnp.float32


def dot(a, b, da, db):
    return lax.dot_general(a, b, (((da,), (db,)), ((), ())), preferred_element_type=f32)


def share(x, axes, n):
    copies = jnp.broadcast_to(x[None], (n,) + x.shape).reshape(n * x.shape[0], x.shape[1])
    return lax.all_to_all(copies, axes, 0, 0, tiled=True)


def gather_lat(x):
    x = share(x, "z", Z)
    x = lax.all_gather(x, "xl", axis=0, tiled=True)
    return lax.all_gather(x, "c", axis=0, tiled=True)


def halve(x, axis):
    half = x.shape[0] // 2
    me = lax.axis_index(axis)
    send = lax.dynamic_slice_in_dim(x, (1 - me) * half, half, 0).astype(bf16)
    keep = lax.dynamic_slice_in_dim(x, me * half, half, 0)
    both = lax.all_gather(send, axis, axis=0, tiled=False)
    return keep + lax.dynamic_index_in_dim(both, 1 - me, 0, keepdims=False).astype(f32)


def scatter_lat(x):
    x = halve(x, "c")
    x = halve(x, "xl")
    parts = lax.all_to_all(x.astype(bf16), "z", 0, 0, tiled=True)
    return jnp.sum(parts.reshape(Z, -1, x.shape[1]).astype(f32), axis=0)


def scatter_tok(x):
    parts = lax.all_to_all(x, TOK, 0, 0, tiled=True)
    return parts.reshape(N_TOK, -1, x.shape[1])


def split2(v):
    high = v.astype(bf16)
    return high, (v - high.astype(f32)).astype(bf16)


def local(inputs, targets, enc_weight, enc_bias, dec_weight, dec_bias):
    rows, width = inputs.shape
    total_rows = rows * Z * XL * C
    full_width = width * N_TOK
    scale_root = math.sqrt(total_rows)

    every_row = gather_lat(inputs)
    pre = dot(every_row, enc_weight, 1, 0).astype(bf16)
    preact = jnp.sum(scatter_tok(pre).astype(f32), axis=0) + enc_bias
    lifted = jnp.maximum(preact, 0.0)
    latent = lifted * lifted
    latent_sum = jnp.sum(latent)
    latent_low = share(latent.astype(bf16), TOK, N_TOK)

    recon = scatter_lat(dot(latent_low, dec_weight, 1, 0)) + dec_bias
    residual = recon - targets.astype(f32)
    grad_recon = (residual / scale_root).astype(bf16)
    row_loss = 0.5 * jnp.sum(residual * residual, axis=1, keepdims=True) + (
        sparsity / rows
    ) * latent_sum
    high, low = split2(row_loss)
    lane = lax.broadcasted_iota(jnp.int32, (rows, 128), 1)
    zero = jnp.zeros((rows, 128), bf16)
    extra = jnp.where(lane == 0, high, jnp.where(lane == 1, low, zero))
    gathered = gather_lat(jnp.concatenate([grad_recon, extra], axis=1))
    every_grad = gathered[:, :width]
    lat_loss = jnp.sum(gathered[:, width:].astype(f32))
    grad_dec_bias = jnp.sum(every_grad.astype(f32), axis=0)

    back = dot(every_grad, dec_weight, 1, 1).astype(bf16)
    back_grad = jnp.sum(scatter_tok(back).astype(f32), axis=0) + sparsity / scale_root
    grad_pre = back_grad * (2.0 * lifted)
    grad_dec = dot(latent_low, every_grad, 0, 0).astype(bf16)

    lats = grad_pre.shape[1]
    high, low = split2(lat_loss)
    bias_high, bias_low = split2(jnp.sum(grad_pre, axis=0, keepdims=True))
    row = lax.broadcasted_iota(jnp.int32, (8, lats), 0)
    zero = jnp.zeros((8, lats), bf16)
    tail = jnp.where(row == 0, bias_high, jnp.where(row == 1, bias_low, zero))
    tail = jnp.where(row == 2, high, jnp.where(row == 3, low, tail))
    shared = share(
        jnp.concatenate([grad_pre.astype(bf16), tail], axis=0), TOK, N_TOK
    ).reshape(N_TOK, -1, lats)
    part = shared.shape[1] - 8
    grad_pre_low = shared[:, :part].reshape(-1, lats)
    tails = jnp.sum(shared[:, part:].astype(f32), axis=0)
    grad_enc_bias = tails[0] + tails[1]
    loss = (tails[2, 0] + tails[3, 0]) / (total_rows * full_width)
    grad_enc = dot(every_row, grad_pre_low, 0, 0).astype(bf16)
    return (loss, grad_enc, grad_dec, grad_enc_bias, grad_dec_bias)


def solution(mesh):
    fine = Mesh(mesh.devices.reshape(Z, XL, C, XH, Y), LAT + TOK)
    in_specs = (
        P(LAT, TOK),
        P(LAT, TOK),
        P(TOK, LAT),
        P(LAT),
        P(LAT, TOK),
        P(TOK),
    )
    out_specs = (P(), P(TOK, LAT), P(LAT, TOK), P(LAT), P(TOK))
    return jax.shard_map(local, mesh=fine, in_specs=in_specs, out_specs=out_specs, check_vma=False)
```

```python
import math

import jax
import jax.numpy as jnp
from jax import lax
from jax.sharding import Mesh, PartitionSpec as P

sparsity = 0.03

SIZES = (4, 4, 2, 2, 2, 4)
ZH, ZL, XL, C, XH, Y = SIZES
LAT = ("zh", "zl", "xl", "c")
TOK = ("xh", "y")
N_TOK = XH * Y
bf16, f32 = jnp.bfloat16, jnp.float32
SWAP = [(0, 1), (1, 0)]


def dot(a, b, da, db):
    return lax.dot_general(a, b, (((da,), (db,)), ((), ())), preferred_element_type=f32)


def exchange(x, axes, n):
    parts = lax.all_to_all(x, axes, 0, 0, tiled=True)
    return parts.reshape(n, x.shape[0] // n, x.shape[1])


def share(x, axes, n):
    copies = jnp.broadcast_to(x[None], (n,) + x.shape).reshape(n * x.shape[0], x.shape[1])
    return exchange(copies, axes, n)


def pick(pair, which):
    return lax.dynamic_index_in_dim(pair, which, 0, keepdims=False)


def partner(x):
    return lax.ppermute(x, "xh", SWAP)


def together(*values):
    return lax.optimization_barrier(values)


def split2(v):
    high = v.astype(bf16)
    return high, (v - high.astype(f32)).astype(bf16)


def fold(x):
    x = jnp.sum(x.reshape(-1, 8, x.shape[1]), axis=0)
    return sum(x[:, i : i + 128] for i in range(0, x.shape[1], 128))


def with_lanes(x, tile):
    high, low = split2(tile)
    rest = jnp.zeros((x.shape[0] - 16, 128), bf16)
    return jnp.concatenate([x.astype(bf16), jnp.concatenate([high, low, rest], axis=0)], axis=1)


def local(inputs, targets, enc_weight, enc_bias, dec_weight, dec_bias):
    rows, width = inputs.shape
    lats = enc_weight.shape[1]
    total_rows = rows * ZH * ZL * XL * C
    full_width = width * N_TOK
    scale_root = math.sqrt(total_rows)
    xh, c, zh = lax.axis_index("xh"), lax.axis_index("c"), lax.axis_index("zh")

    dec_other = partner(dec_weight)
    x = share(inputs, ("zl", "zh"), ZL * ZH).reshape(-1, width)
    x = lax.all_gather(x, "xl", axis=0, tiled=True)
    x, dec_other = together(x, dec_other)
    every_row = lax.all_gather(x, "c", axis=0, tiled=True)
    pre = dot(every_row, enc_weight, 1, 0).astype(bf16)
    pre_parts = exchange(pre, TOK, N_TOK)
    my_target = lax.ppermute(
        targets.astype(f32) - dec_bias, ("c", "xh"), [(0, 0), (1, 2), (2, 1), (3, 3)]
    )
    pre_parts, my_target = together(pre_parts, my_target)
    preact = jnp.sum(pre_parts.astype(f32), axis=0) + enc_bias
    lifted = jnp.maximum(preact, 0.0)
    latent = lifted * lifted
    latent_sum = fold(latent)
    latent_low = lax.all_gather(latent.astype(bf16), "y", axis=0, tiled=True)

    same = c == xh
    recon_mine = dot(latent_low, dec_weight, 1, 0)
    recon_other = dot(latent_low, dec_other, 1, 0)
    send = jnp.where(same, recon_other, recon_mine).astype(bf16)
    both = lax.all_gather(send, "c", axis=0, tiled=False)
    part = jnp.where(same, recon_mine, recon_other) + pick(both, 1 - c).astype(f32)
    part = jnp.sum(exchange(part.astype(bf16), ("xl", "zl"), XL * ZL).astype(f32), axis=0)
    block = lax.broadcasted_iota(jnp.int32, (ZH, rows, width), 0)
    minus = jnp.where(block == zh, my_target[None], 0.0).reshape(ZH * rows, width)
    every = share(with_lanes(part - minus, latent_sum), "zh", ZH)
    every, lat_other = together(every, partner(latent_low))
    every = jnp.sum(every.astype(f32), axis=0)
    residual = every[:, :width]
    piece = 0.5 * fold(residual * residual) + sparsity * fold(every[:, width:])
    grad = with_lanes(residual / scale_root, piece)
    grad = share(grad, ("xl", "zl"), XL * ZL).reshape(-1, width + 128)
    grad = lax.all_gather(grad, "c", axis=0, tiled=False)
    lat_loss = jnp.sum(grad[:, :, width:].astype(f32))
    grad_mine = pick(grad, xh)[:, :width]
    grad_send = pick(grad, 1 - xh)[:, :width]

    back = (dot(grad_mine, dec_weight, 1, 1) + dot(grad_send, dec_other, 1, 1)).astype(bf16)
    back_parts, grad_recv = together(exchange(back, "y", Y), partner(grad_send))
    back_grad = jnp.sum(back_parts.astype(f32), axis=0) + sparsity / scale_root
    grad_dec_bias = jnp.sum(grad_mine.astype(f32), axis=0) + jnp.sum(
        grad_recv.astype(f32), axis=0
    )
    grad_dec = (dot(latent_low, grad_mine, 0, 0) + dot(lat_other, grad_recv, 0, 0)).astype(bf16)
    grad_pre = back_grad * (2.0 * lifted)

    high, low = split2(lat_loss)
    bias_high, bias_low = split2(jnp.sum(grad_pre, axis=0, keepdims=True))
    row = lax.broadcasted_iota(jnp.int32, (8, lats), 0)
    zero = jnp.zeros((8, lats), bf16)
    tail = jnp.where(row == 0, bias_high, jnp.where(row == 1, bias_low, zero))
    tail = jnp.where(row == 2, high, jnp.where(row == 3, low, tail))
    shared = share(jnp.concatenate([grad_pre.astype(bf16), tail], axis=0), TOK, N_TOK)
    slab = shared.shape[1] - 8
    grad_pre_low = shared[:, :slab].reshape(-1, lats)
    tails = jnp.sum(shared[:, slab:].astype(f32), axis=0)
    grad_enc_bias = tails[0] + tails[1]
    loss = (tails[2, 0] + tails[3, 0]) / (total_rows * full_width)
    grad_enc = dot(every_row, grad_pre_low, 0, 0).astype(bf16)
    return (loss, grad_enc, grad_dec, grad_enc_bias, grad_dec_bias)


def solution(mesh):
    fine = Mesh(mesh.devices.reshape(SIZES), LAT + TOK)
    in_specs = (
        P(LAT, TOK),
        P(LAT, TOK),
        P(TOK, LAT),
        P(LAT),
        P(LAT, TOK),
        P(TOK),
    )
    out_specs = (P(), P(TOK, LAT), P(LAT, TOK), P(LAT), P(TOK))
    return jax.shard_map(local, mesh=fine, in_specs=in_specs, out_specs=out_specs, check_vma=False)
```

```python
import math

import jax
import jax.numpy as jnp
from jax import lax
from jax.sharding import Mesh, PartitionSpec as P

sparsity = 0.03

SIZES = (4, 4, 2, 2, 2, 4)
ZH, ZL, XL, C, XH, Y = SIZES
LAT = ("zh", "zl", "xl", "c")
TOK = ("xh", "y")
N_TOK = XH * Y
bf16, f32 = jnp.bfloat16, jnp.float32
SWAP = [(0, 1), (1, 0)]


def dot(a, b, da, db):
    return lax.dot_general(a, b, (((da,), (db,)), ((), ())), preferred_element_type=f32)


def exchange(x, axes, n):
    parts = lax.all_to_all(x, axes, 0, 0, tiled=True)
    return parts.reshape(n, x.shape[0] // n, x.shape[1])


def share(x, axes, n):
    copies = jnp.broadcast_to(x[None], (n,) + x.shape).reshape(n * x.shape[0], x.shape[1])
    return exchange(copies, axes, n)


def pick(pair, which):
    return lax.dynamic_index_in_dim(pair, which, 0, keepdims=False)


def partner(x):
    return lax.ppermute(x, "xh", SWAP)


def together(*values):
    return lax.optimization_barrier(values)


def split2(v):
    high = v.astype(bf16)
    return high, (v - high.astype(f32)).astype(bf16)


def fold(x):
    x = jnp.sum(x.reshape(-1, 8, x.shape[1]), axis=0)
    return sum(x[:, i : i + 128] for i in range(0, x.shape[1], 128))


def with_lanes(x, tile):
    high, low = split2(tile)
    rest = jnp.zeros((x.shape[0] - 16, 128), bf16)
    return jnp.concatenate([x.astype(bf16), jnp.concatenate([high, low, rest], axis=0)], axis=1)


def local(inputs, targets, enc_weight, enc_bias, dec_weight, dec_bias):
    rows, width = inputs.shape
    lats = enc_weight.shape[1]
    total_rows = rows * ZH * ZL * XL * C
    full_width = width * N_TOK
    scale_root = math.sqrt(total_rows)
    xh, c, zh = lax.axis_index("xh"), lax.axis_index("c"), lax.axis_index("zh")

    dec_other = partner(dec_weight)
    x = share(inputs, ("zl", "zh"), ZL * ZH).reshape(-1, width)
    x = lax.all_gather(x, "xl", axis=0, tiled=True)
    x, dec_other = together(x, dec_other)
    every_row = lax.all_gather(x, "c", axis=0, tiled=True)
    pre = dot(every_row, enc_weight, 1, 0).astype(bf16)
    pre_parts = exchange(pre, TOK, N_TOK)
    my_target = lax.ppermute(
        targets.astype(f32) - dec_bias, ("c", "xh"), [(0, 0), (1, 2), (2, 1), (3, 3)]
    )
    pre_parts, my_target = together(pre_parts, my_target)
    preact = jnp.sum(pre_parts.astype(f32), axis=0) + enc_bias
    lifted = jnp.maximum(preact, 0.0)
    latent = lifted * lifted
    latent_sum = fold(latent)
    latent_low = lax.all_gather(latent.astype(bf16), "y", axis=0, tiled=True)

    same = c == xh
    recon_mine = dot(latent_low, dec_weight, 1, 0)
    recon_other = dot(latent_low, dec_other, 1, 0)
    send = jnp.where(same, recon_other, recon_mine).astype(bf16)
    both = lax.all_gather(send, "c", axis=0, tiled=False)
    part = jnp.where(same, recon_mine, recon_other) + pick(both, 1 - c).astype(f32)
    part = jnp.sum(exchange(part.astype(bf16), ("xl", "zl"), XL * ZL).astype(f32), axis=0)
    block = lax.broadcasted_iota(jnp.int32, (ZH, rows, width), 0)
    minus = jnp.where(block == zh, my_target[None], 0.0).reshape(ZH * rows, width)
    every = share(with_lanes(part - minus, latent_sum), "zh", ZH)
    every, lat_other = together(every, partner(latent_low))
    every = jnp.sum(every.astype(f32), axis=0)
    residual = every[:, :width]
    piece = 0.5 * fold(residual * residual) + sparsity * fold(every[:, width:])
    grad = with_lanes(residual / scale_root, piece)
    grad = share(grad, ("xl", "zl"), XL * ZL).reshape(-1, width + 128)
    grad = lax.all_gather(grad, "c", axis=0, tiled=False)
    lat_loss = jnp.sum(grad[:, :, width:].astype(f32))
    grad_mine = pick(grad, xh)[:, :width]
    grad_send = pick(grad, 1 - xh)[:, :width]

    back = (dot(grad_mine, dec_weight, 1, 1) + dot(grad_send, dec_other, 1, 1)).astype(bf16)
    fetch = pick(grad_send.reshape(2, -1, width), lax.axis_index("c"))
    back_parts, grad_recv = together(exchange(back, "y", Y), partner(fetch))
    grad_recv = lax.all_gather(grad_recv, "c", axis=0, tiled=True)
    back_grad = jnp.sum(back_parts.astype(f32), axis=0) + sparsity / scale_root
    grad_dec_bias = jnp.sum(grad_mine.astype(f32), axis=0) + jnp.sum(
        grad_recv.astype(f32), axis=0
    )
    grad_dec = (dot(latent_low, grad_mine, 0, 0) + dot(lat_other, grad_recv, 0, 0)).astype(bf16)
    grad_pre = back_grad * (2.0 * lifted)

    high, low = split2(lat_loss)
    bias_high, bias_low = split2(jnp.sum(grad_pre, axis=0, keepdims=True))
    row = lax.broadcasted_iota(jnp.int32, (8, lats), 0)
    zero = jnp.zeros((8, lats), bf16)
    tail = jnp.where(row == 0, bias_high, jnp.where(row == 1, bias_low, zero))
    tail = jnp.where(row == 2, high, jnp.where(row == 3, low, tail))
    shared = share(jnp.concatenate([grad_pre.astype(bf16), tail], axis=0), TOK, N_TOK)
    slab = shared.shape[1] - 8
    grad_pre_low = shared[:, :slab].reshape(-1, lats)
    tails = jnp.sum(shared[:, slab:].astype(f32), axis=0)
    grad_enc_bias = tails[0] + tails[1]
    loss = (tails[2, 0] + tails[3, 0]) / (total_rows * full_width)
    grad_enc = dot(every_row, grad_pre_low, 0, 0).astype(bf16)
    return (loss, grad_enc, grad_dec, grad_enc_bias, grad_dec_bias)


def solution(mesh):
    fine = Mesh(mesh.devices.reshape(SIZES), LAT + TOK)
    in_specs = (
        P(LAT, TOK),
        P(LAT, TOK),
        P(TOK, LAT),
        P(LAT),
        P(LAT, TOK),
        P(TOK),
    )
    out_specs = (P(), P(TOK, LAT), P(LAT, TOK), P(LAT), P(TOK))
    return jax.shard_map(local, mesh=fine, in_specs=in_specs, out_specs=out_specs, check_vma=False)
```

```python
import math

import jax
import jax.numpy as jnp
from jax import lax
from jax.sharding import Mesh, PartitionSpec as P

sparsity = 0.03

SIZES = (4, 4, 2, 2, 2, 4)
ZH, ZL, XL, C, XH, Y = SIZES
LAT = ("zh", "zl", "xl", "c")
TOK = ("xh", "y")
N_TOK = XH * Y
bf16, f32 = jnp.bfloat16, jnp.float32
SWAP = [(0, 1), (1, 0)]


def dot(a, b, da, db):
    return lax.dot_general(a, b, (((da,), (db,)), ((), ())), preferred_element_type=f32)


def exchange(x, axes, n):
    parts = lax.all_to_all(x, axes, 0, 0, tiled=True)
    return parts.reshape(n, x.shape[0] // n, x.shape[1])


def share(x, axes, n):
    copies = jnp.broadcast_to(x[None], (n,) + x.shape).reshape(n * x.shape[0], x.shape[1])
    return exchange(copies, axes, n)


def pick(pair, which):
    return lax.dynamic_index_in_dim(pair, which, 0, keepdims=False)


def partner(x):
    return lax.ppermute(x, "xh", SWAP)


def together(*values):
    return lax.optimization_barrier(values)


def split2(v):
    high = v.astype(bf16)
    return high, (v - high.astype(f32)).astype(bf16)


def fold(x):
    x = jnp.sum(x.reshape(-1, 8, x.shape[1]), axis=0)
    return sum(x[:, i : i + 128] for i in range(0, x.shape[1], 128))


def with_lanes(x, tile):
    high, low = split2(tile)
    rest = jnp.zeros((x.shape[0] - 16, 128), bf16)
    return jnp.concatenate([x.astype(bf16), jnp.concatenate([high, low, rest], axis=0)], axis=1)


def local(inputs, targets, enc_weight, enc_bias, dec_weight, dec_bias):
    rows, width = inputs.shape
    lats = enc_weight.shape[1]
    total_rows = rows * ZH * ZL * XL * C
    full_width = width * N_TOK
    scale_root = math.sqrt(total_rows)
    xh, c, zh = lax.axis_index("xh"), lax.axis_index("c"), lax.axis_index("zh")

    dec_other = partner(dec_weight)
    x = share(inputs, ("zl", "zh"), ZL * ZH).reshape(-1, width)
    x = lax.all_gather(x, "xl", axis=0, tiled=True)
    x, dec_other = together(x, dec_other)
    every_row = lax.all_gather(x, "c", axis=0, tiled=True)
    pre = dot(every_row, enc_weight, 1, 0).astype(bf16)
    pre_parts = exchange(pre, TOK, N_TOK)
    my_target = lax.ppermute(
        targets.astype(f32) - dec_bias, ("c", "xh"), [(0, 0), (1, 2), (2, 1), (3, 3)]
    )
    same = c == xh
    dec_pair = jnp.where(
        same, jnp.stack([dec_weight, dec_other]), jnp.stack([dec_other, dec_weight])
    )
    pre_parts, my_target, dec_pair = together(pre_parts, my_target, dec_pair)
    preact = jnp.sum(pre_parts.astype(f32), axis=0) + enc_bias
    lifted = jnp.maximum(preact, 0.0)
    latent = lifted * lifted
    latent_sum = fold(latent)
    latent_low = lax.all_gather(latent.astype(bf16), "y", axis=0, tiled=True)

    send = dot(latent_low, dec_pair[1], 1, 0).astype(bf16)
    both = lax.all_gather(send, "c", axis=0, tiled=False)
    part = dot(latent_low, dec_pair[0], 1, 0) + pick(both, 1 - c).astype(f32)
    part = jnp.sum(exchange(part.astype(bf16), ("xl", "zl"), XL * ZL).astype(f32), axis=0)
    block = lax.broadcasted_iota(jnp.int32, (ZH, rows, width), 0)
    minus = jnp.where(block == zh, my_target[None], 0.0).reshape(ZH * rows, width)
    every = share(with_lanes(part - minus, latent_sum), "zh", ZH)
    every, lat_other = together(every, partner(latent_low))
    every = jnp.sum(every.astype(f32), axis=0)
    residual = every[:, :width]
    piece = 0.5 * fold(residual * residual) + sparsity * fold(every[:, width:])
    grad = with_lanes(residual / scale_root, piece)
    grad = share(grad, ("xl", "zl"), XL * ZL).reshape(-1, width + 128)
    grad = lax.all_gather(grad, "c", axis=0, tiled=False)
    lat_loss = jnp.sum(grad[:, :, width:].astype(f32))
    grad_mine = pick(grad, xh)[:, :width]
    grad_send = pick(grad, 1 - xh)[:, :width]

    back = (dot(grad_mine, dec_weight, 1, 1) + dot(grad_send, dec_other, 1, 1)).astype(bf16)
    fetch = pick(grad_send.reshape(2, -1, width), lax.axis_index("c"))
    back_parts, grad_recv = together(exchange(back, "y", Y), partner(fetch))
    grad_recv = lax.all_gather(grad_recv, "c", axis=0, tiled=True)
    back_grad = jnp.sum(back_parts.astype(f32), axis=0) + sparsity / scale_root
    grad_dec_bias = jnp.sum(grad_mine.astype(f32), axis=0) + jnp.sum(
        grad_recv.astype(f32), axis=0
    )
    grad_dec = (dot(latent_low, grad_mine, 0, 0) + dot(lat_other, grad_recv, 0, 0)).astype(bf16)
    grad_pre = back_grad * (2.0 * lifted)

    high, low = split2(lat_loss)
    bias_high, bias_low = split2(jnp.sum(grad_pre, axis=0, keepdims=True))
    row = lax.broadcasted_iota(jnp.int32, (8, lats), 0)
    zero = jnp.zeros((8, lats), bf16)
    tail = jnp.where(row == 0, bias_high, jnp.where(row == 1, bias_low, zero))
    tail = jnp.where(row == 2, high, jnp.where(row == 3, low, tail))
    shared = share(jnp.concatenate([grad_pre.astype(bf16), tail], axis=0), TOK, N_TOK)
    slab = shared.shape[1] - 8
    grad_pre_low = shared[:, :slab].reshape(-1, lats)
    tails = jnp.sum(shared[:, slab:].astype(f32), axis=0)
    grad_enc_bias = tails[0] + tails[1]
    loss = (tails[2, 0] + tails[3, 0]) / (total_rows * full_width)
    grad_enc = dot(every_row, grad_pre_low, 0, 0).astype(bf16)
    return (loss, grad_enc, grad_dec, grad_enc_bias, grad_dec_bias)


def solution(mesh):
    fine = Mesh(mesh.devices.reshape(SIZES), LAT + TOK)
    in_specs = (
        P(LAT, TOK),
        P(LAT, TOK),
        P(TOK, LAT),
        P(LAT),
        P(LAT, TOK),
        P(TOK),
    )
    out_specs = (P(), P(TOK, LAT), P(LAT, TOK), P(LAT), P(TOK))
    return jax.shard_map(local, mesh=fine, in_specs=in_specs, out_specs=out_specs, check_vma=False)
```

```python
import math

import jax
import jax.numpy as jnp
from jax import lax
from jax.sharding import Mesh, PartitionSpec as P

sparsity = 0.03

SIZES = (4, 4, 2, 2, 2, 4)
ZH, ZL, XL, C, XH, Y = SIZES
LAT = ("zh", "zl", "xl", "c")
TOK = ("xh", "y")
N_TOK = XH * Y
bf16, f32 = jnp.bfloat16, jnp.float32
SWAP = [(0, 1), (1, 0)]


def dot(a, b, da, db):
    return lax.dot_general(a, b, (((da,), (db,)), ((), ())), preferred_element_type=f32)


def exchange(x, axes, n):
    parts = lax.all_to_all(x, axes, 0, 0, tiled=True)
    return parts.reshape(n, x.shape[0] // n, x.shape[1])


def share(x, axes, n):
    copies = jnp.broadcast_to(x[None], (n,) + x.shape).reshape(n * x.shape[0], x.shape[1])
    return exchange(copies, axes, n)


def pick(pair, which):
    return lax.dynamic_index_in_dim(pair, which, 0, keepdims=False)


def partner(x):
    return lax.ppermute(x, "xh", SWAP)


def together(*values):
    return lax.optimization_barrier(values)


def split2(v):
    high = v.astype(bf16)
    return high, (v - high.astype(f32)).astype(bf16)


def fold(x):
    x = jnp.sum(x.reshape(-1, 8, x.shape[1]), axis=0)
    return sum(x[:, i : i + 128] for i in range(0, x.shape[1], 128))


def with_lanes(x, tile):
    high, low = split2(tile)
    rest = jnp.zeros((x.shape[0] - 16, 128), bf16)
    return jnp.concatenate([x.astype(bf16), jnp.concatenate([high, low, rest], axis=0)], axis=1)


def local(inputs, targets, enc_weight, enc_bias, dec_weight, dec_bias):
    rows, width = inputs.shape
    lats = enc_weight.shape[1]
    total_rows = rows * ZH * ZL * XL * C
    full_width = width * N_TOK
    scale_root = math.sqrt(total_rows)
    xh, c, zh = lax.axis_index("xh"), lax.axis_index("c"), lax.axis_index("zh")

    dec_other = partner(dec_weight)
    x = share(inputs, ("zl", "zh"), ZL * ZH).reshape(-1, width)
    x = lax.all_gather(x, "xl", axis=0, tiled=True)
    every_row = lax.all_gather(x, "c", axis=0, tiled=True)
    every_row, dec_other = together(every_row, dec_other)
    pre = dot(every_row, enc_weight, 1, 0).astype(bf16)
    pre_parts = exchange(pre, TOK, N_TOK)
    my_target = lax.ppermute(
        targets.astype(f32) - dec_bias, ("c", "xh"), [(0, 0), (1, 2), (2, 1), (3, 3)]
    )
    same = c == xh
    dec_pair = jnp.where(
        same, jnp.stack([dec_weight, dec_other]), jnp.stack([dec_other, dec_weight])
    )
    pre_parts, my_target, dec_pair = together(pre_parts, my_target, dec_pair)
    preact = jnp.sum(pre_parts.astype(f32), axis=0) + enc_bias
    lifted = jnp.maximum(preact, 0.0)
    latent = lifted * lifted
    latent_sum = fold(latent)
    latent_low = lax.all_gather(latent.astype(bf16), "y", axis=0, tiled=True)

    send = dot(latent_low, dec_pair[1], 1, 0).astype(bf16)
    both = lax.all_gather(send, "c", axis=0, tiled=False)
    part = dot(latent_low, dec_pair[0], 1, 0) + pick(both, 1 - c).astype(f32)
    part = jnp.sum(exchange(part.astype(bf16), ("xl", "zl"), XL * ZL).astype(f32), axis=0)
    block = lax.broadcasted_iota(jnp.int32, (ZH, rows, width), 0)
    minus = jnp.where(block == zh, my_target[None], 0.0).reshape(ZH * rows, width)
    every = share(with_lanes(part - minus, latent_sum), "zh", ZH)
    every, lat_other = together(every, partner(latent_low))
    every = jnp.sum(every.astype(f32), axis=0)
    residual = every[:, :width]
    piece = 0.5 * fold(residual * residual) + sparsity * fold(every[:, width:])
    grad = with_lanes(residual / scale_root, piece)
    grad = share(grad, ("xl", "zl"), XL * ZL).reshape(-1, width + 128)
    grad = lax.all_gather(grad, "c", axis=0, tiled=False)
    lat_loss = jnp.sum(grad[:, :, width:].astype(f32))
    grad_mine = pick(grad, xh)[:, :width]
    grad_send = pick(grad, 1 - xh)[:, :width]

    back = (dot(grad_mine, dec_weight, 1, 1) + dot(grad_send, dec_other, 1, 1)).astype(bf16)
    fetch = pick(grad_send.reshape(2, -1, width), lax.axis_index("c"))
    back_parts, grad_recv = together(exchange(back, "y", Y), partner(fetch))
    grad_recv = lax.all_gather(grad_recv, "c", axis=0, tiled=True)
    back_grad = jnp.sum(back_parts.astype(f32), axis=0) + sparsity / scale_root
    grad_dec_bias = jnp.sum(grad_mine.astype(f32), axis=0) + jnp.sum(
        grad_recv.astype(f32), axis=0
    )
    grad_dec = (dot(latent_low, grad_mine, 0, 0) + dot(lat_other, grad_recv, 0, 0)).astype(bf16)
    grad_pre = back_grad * (2.0 * lifted)

    high, low = split2(lat_loss)
    bias_high, bias_low = split2(jnp.sum(grad_pre, axis=0, keepdims=True))
    row = lax.broadcasted_iota(jnp.int32, (8, lats), 0)
    zero = jnp.zeros((8, lats), bf16)
    tail = jnp.where(row == 0, bias_high, jnp.where(row == 1, bias_low, zero))
    tail = jnp.where(row == 2, high, jnp.where(row == 3, low, tail))
    shared = share(jnp.concatenate([grad_pre.astype(bf16), tail], axis=0), TOK, N_TOK)
    slab = shared.shape[1] - 8
    grad_pre_low = shared[:, :slab].reshape(-1, lats)
    tails = jnp.sum(shared[:, slab:].astype(f32), axis=0)
    grad_enc_bias = tails[0] + tails[1]
    loss = (tails[2, 0] + tails[3, 0]) / (total_rows * full_width)
    grad_enc = dot(every_row, grad_pre_low, 0, 0).astype(bf16)
    return (loss, grad_enc, grad_dec, grad_enc_bias, grad_dec_bias)


def solution(mesh):
    fine = Mesh(mesh.devices.reshape(SIZES), LAT + TOK)
    in_specs = (
        P(LAT, TOK),
        P(LAT, TOK),
        P(TOK, LAT),
        P(LAT),
        P(LAT, TOK),
        P(TOK),
    )
    out_specs = (P(), P(TOK, LAT), P(LAT, TOK), P(LAT), P(TOK))
    return jax.shard_map(local, mesh=fine, in_specs=in_specs, out_specs=out_specs, check_vma=False)
```
